32 devices in a mesh: dp: 8 (over z, core), mp: 4 (over y, x).
Axes of the slice: x: 2, y: 2, z: 4, core: 2. Of those that a mesh axis runs over, the one named last changes fastest.
Arguments:
- hidden_in: bfloat16 [16, 512, 8192], P('dp', None, 'mp'), may hold values from -6 to 6
- query_act: bfloat16 [16, 512, 8192], P('dp', None, 'mp'), may hold values from -6 to 6
- key_act: bfloat16 [16, 512, 1024], P('dp'), may hold values from -6 to 6
- value_act: bfloat16 [16, 512, 1024], P('dp'), may hold values from -6 to 6
- ctx_grad: bfloat16 [16, 512, 8192], P('dp', None, 'mp'), may hold values from -6 to 6
- segment_ids: int32 [16, 512], P('dp'), may hold values from 0 to 3, never falling along the last dimension, each value on 1 to 256 neighbouring positions
- down_query: bfloat16 [8192, 128], P('mp'), may hold values from -0.0625 to 0.0625
- up_query: bfloat16 [128, 8192], P(None, 'mp'), may hold values from -0.5 to 0.5
- down_value: bfloat16 [8192, 128], P('mp'), may hold values from -0.0625 to 0.0625
- up_value: bfloat16 [128, 1024], replicated, may hold values from -0.5 to 0.5
- block_rows: int32 [3, 8192], P(None, 'mp'), may hold values from 0 to 63
- tile_rows: int32 [3, 8192], P(None, 'mp'), may hold values from 0 to 7
- block_value: int32 [1024], replicated, may hold values from 0 to 63
- tile_value: int32 [1024], replicated, may hold values from 0 to 7
- tile_bank: bfloat16 [8, 128, 128], replicated, may hold values from -0.5 to 0.5
- seed_feats: bfloat16 [256, 8192], P('dp', 'mp'), may hold values from -6 to 6
Outputs:
- scores: float32 [16, 256], P('dp', 'mp')
The draws below stay inside these ranges and needn't reach their ends.
All inputs are finite; a program needn't handle non-finite values.
Results may differ from the reference program's by a relative error of at most 0.022.
Values may be sent and summed in bfloat16 or wider, within the bound.
A program may use at most 192 MiB of HBM per device.

```python
import math
import jax
import jax.numpy as jnp
import numpy as np
from jax import lax

D = 8192
H = 64
KVH = 8
DH = 128
R = 128
K = 8192
PB = 128
NT = 8
S = 512
KB = 64
CANDS = 16
SEEDS = 256


def base_draw(key, full_shape):
    return jax.random.truncated_normal(key, -5.5, 5.5, full_shape, jnp.float32)


def draw_query_act(key, part):
    values_out = base_draw(jax.random.fold_in(key, 1), (CANDS, S, H, DH))
    return values_out.reshape(CANDS, S, H * DH).astype(jnp.bfloat16)


def draw_key_act(key, part):
    values_out = base_draw(jax.random.fold_in(key, 2), (CANDS, S, KVH, DH))
    return values_out.reshape(CANDS, S, KVH * DH).astype(jnp.bfloat16)


def with_ends(result, own_key, low, largest):
    longest = result.shape.index(max(result.shape))
    spots = []
    for shift in (0, 1):
        where = [jax.random.randint(jax.random.fold_in(own_key, axis), (), 0, length) for axis, length in enumerate(result.shape)]
        where[longest] = (where[longest] + shift) % result.shape[longest]
        spots.append(tuple(where))
    return result.at[spots[0]].set(low).at[spots[1]].set(largest)


def shard_levels(key, dims, shards, low, largest):
    level, own = 1.0, jax.random.fold_in(key, 6)
    for dim, blocks in shards:
        draws = jnp.exp(jax.random.uniform(jax.random.fold_in(own, dim), (blocks,), jnp.float32, low / len(shards), largest / len(shards)))
        level = level * jnp.repeat(draws, dims[dim] // blocks).reshape([-1 if axis == dim else 1 for axis in range(len(dims))])
    return level


def rank_table(number_of, skew):
    portions = [(1 << 20) // math.isqrt(standing ** skew) + 1 for standing in range(1, number_of + 1)]
    width = 1 + sum(portions) // (1 << 30)
    return np.cumsum(np.array([max(1, weight // width) for weight in portions]))


def skewed_ids(stream_key, dims, number_of, skew):
    listing = rank_table(number_of, skew)
    ticket = jax.random.randint(jax.random.fold_in(stream_key, 1), dims, 0, int(listing[number_of - 1]))
    rank = jnp.searchsorted(jnp.asarray(listing, jnp.int32), ticket, side="right")
    return jax.random.permutation(jax.random.fold_in(stream_key, 2), number_of)[rank].astype(jnp.int32)


def split_up(amount, total, reach, slope):
    loads = [(1 << 20) // math.isqrt(rank ** slope) + 1 for rank in range(2, amount + 1)]
    surplus, given = total - reach - (amount - 1), [1] * (amount - 1)
    while surplus > 0:
        candidates = [i for i in range(amount - 1) if given[i] < reach]
        pool, left = sum([loads[i] for i in candidates]), surplus
        for i in candidates:
            more = min(reach - given[i], max(1, left * loads[i] // pool), surplus)
            given[i] = given[i] + more
            surplus = surplus - more
    return np.array([reach] + given)


def uneven_parts(own_key, count, total, limit, lean):
    if count == 2:
        one = jax.random.randint(own_key, (), max(1, total - limit), min(limit, total - 1) + 1)
        return jnp.stack([one, total - one])
    lengths = jnp.asarray(split_up(count, total, limit, lean), jnp.int32)
    pairs = (count - 1) // 2
    source_of, sink = lengths[1:1 + 2 * pairs:2], lengths[2:2 + 2 * pairs:2]
    slack = jnp.minimum(source_of - 1, limit - sink)
    passed = jax.random.randint(jax.random.fold_in(own_key, 1), (pairs,), 0, 1 << 20) % (slack + 1)
    lengths = lengths.at[1:1 + 2 * pairs:2].set(source_of - passed).at[2:2 + 2 * pairs:2].set(sink + passed)
    return lengths[jax.random.permutation(jax.random.fold_in(own_key, 2), count)]


def normal_values(key, shape, width, bound, shards=(), held_as=jnp.bfloat16):
    level = shard_levels(key, shape, shards, -0.22, 0.18) if shards else 1.0
    result = jax.random.normal(key, shape, jnp.float32) * width * level
    return jnp.minimum(jnp.maximum(result, -bound), bound).astype(held_as)


def setup_inputs(seed: int = 0) -> dict:
    seeds = jax.random.split(jax.random.key(seed), 17)
    hidden_in = normal_values(seeds[0], (CANDS, S, D), 1.0, 6.0, ((0, 8), (2, 4)))
    query_act = draw_query_act(jax.random.fold_in(seeds[16], 71), 0)
    key_act = draw_key_act(jax.random.fold_in(seeds[16], 71), 0)
    value_act = normal_values(seeds[3], (CANDS, S, KVH * DH), 1.0, 6.0, ((0, 8),))
    ctx_grad = normal_values(seeds[4], (CANDS, S, H * DH), 1.0, 6.0, ((0, 8), (2, 4)))
    segment_ids = jax.vmap(lambda own: jnp.searchsorted(jnp.cumsum(uneven_parts(own, 4, S, S // 2, 1)), jnp.arange(S), side="right"))(jax.random.split(seeds[5], CANDS)).reshape((CANDS, S)).astype(jnp.int32)
    down_query = normal_values(seeds[6], (D, R), D ** -0.5, 0.0625, ((0, 4),))
    up_query = normal_values(seeds[7], (R, H * DH), R ** -0.5, 0.5, ((1, 4),))
    down_value = normal_values(seeds[8], (D, R), D ** -0.5, 0.0625, ((0, 4),))
    up_value = normal_values(seeds[9], (R, KVH * DH), R ** -0.5, 0.5)
    block_rows = with_ends(skewed_ids(seeds[10], (3, D), KB, 2), jax.random.fold_in(seeds[10], 3), 0, KB - 1).astype(jnp.int32)
    tile_rows = with_ends(jax.random.randint(seeds[11], (3, D), 0, NT), jax.random.fold_in(seeds[11], 1), 0, NT - 1).astype(jnp.int32)
    block_value = with_ends(skewed_ids(seeds[12], (KVH * DH,), KB, 2), jax.random.fold_in(seeds[12], 3), 0, KB - 1).astype(jnp.int32)
    tile_value = with_ends(jax.random.randint(seeds[13], (KVH * DH,), 0, NT), jax.random.fold_in(seeds[13], 1), 0, NT - 1).astype(jnp.int32)
    tile_bank = normal_values(seeds[14], (NT, R, PB), R ** -0.5, 0.5)
    seed_feats = normal_values(seeds[15], (SEEDS, K), 1.0, 6.0, ((0, 8), (1, 4)))
    return dict(hidden_in=hidden_in, query_act=query_act, key_act=key_act, value_act=value_act, ctx_grad=ctx_grad, segment_ids=segment_ids, down_query=down_query, up_query=up_query, down_value=down_value, up_value=up_value, block_rows=block_rows, tile_rows=tile_rows, block_value=block_value, tile_value=tile_value, tile_bank=tile_bank, seed_feats=seed_feats)


EPS = 1e-06

def rounded(value):
    return lax.optimization_barrier(value.astype(jnp.bfloat16)).astype(jnp.float32)

def reference(hidden_in, query_act, key_act, value_act, ctx_grad, segment_ids, down_query, up_query, down_value, up_value, block_rows, tile_rows, block_value, tile_value, tile_bank, seed_feats):
    head_group = H // KVH
    score_scale = 1.0 / math.sqrt(DH)
    both_down = jnp.concatenate([down_query, down_value], axis=1)
    bucket_ids = jnp.concatenate([(block_rows * NT + tile_rows).reshape(-1), block_value * NT + tile_value]).astype(jnp.int32)
    tile_table = tile_bank.astype(jnp.float32).reshape(NT * R, PB)
    position = jnp.arange(S, dtype=jnp.int32)
    causal = position[None, :] <= position[:, None]
    up_three = up_value.astype(jnp.float32).reshape(R, KVH, DH)

    def features(inputs):
        hidden, query, keyed, valued, grad_out, segment = inputs
        allowed = causal & (segment[:, None] == segment[None, :])
        lowrank_in = jnp.dot(hidden, both_down, preferred_element_type=jnp.float32).astype(jnp.bfloat16)
        query_h = query.reshape(S, H, DH).astype(jnp.float32)
        key_h = jnp.repeat(keyed.reshape(S, KVH, DH), head_group, axis=1).astype(jnp.float32)
        value_h = jnp.repeat(valued.reshape(S, KVH, DH), head_group, axis=1).astype(jnp.float32)
        grad_h = grad_out.reshape(S, H, DH).astype(jnp.float32)
        logits = jnp.einsum('qhd,khd->hqk', query_h, key_h) * score_scale
        logits = jnp.where(allowed[None], logits, -1e+30)
        row_top = lax.optimization_barrier(jnp.max(logits, axis=-1, keepdims=True))
        exp_terms = jnp.exp(logits - row_top)
        attn_probs = exp_terms / lax.optimization_barrier(jnp.sum(exp_terms, axis=-1, keepdims=True))
        value_grad = jnp.einsum('hqk,qhd->khd', rounded(attn_probs), grad_h).astype(jnp.bfloat16)
        prob_grad = jnp.einsum('qhd,khd->hqk', grad_h, value_h)
        row_delta = lax.optimization_barrier(jnp.sum(attn_probs * prob_grad, axis=-1, keepdims=True))
        logit_grad = rounded(attn_probs * (prob_grad - row_delta))
        query_grad = (jnp.einsum('hqk,khd->qhd', logit_grad, key_h) * score_scale).astype(jnp.bfloat16)
        query_flat = query_grad.reshape(S, H * DH)
        value_five = value_grad.reshape(S, KVH, head_group, DH).astype(jnp.float32)
        back_query = jnp.dot(query_flat, up_query.T, preferred_element_type=jnp.float32)
        back_value = jnp.einsum('skgd,rkd->sr', value_five, up_three)
        lowrank_back = jnp.concatenate([back_query, back_value], axis=1).astype(jnp.bfloat16)
        grad_down = jnp.dot(hidden.T, lowrank_back, preferred_element_type=jnp.float32)
        grad_upq = jnp.dot(lowrank_in[:, :R].T, query_flat, preferred_element_type=jnp.float32)
        grad_upv = jnp.einsum('sr,skgd->rkd', lowrank_in[:, R:].astype(jnp.float32), value_five).reshape(R, KVH * DH)
        grad_rows = jnp.concatenate([grad_down[:, :R], grad_down[:, R:], grad_upq.T, grad_upv.T], axis=0)
        block_sums = jax.ops.segment_sum(grad_rows, bucket_ids, num_segments=KB * NT)
        projected = jnp.dot(block_sums.reshape(KB, NT * R), tile_table, precision=lax.Precision.HIGHEST)
        return projected.reshape(K)
    feats = lax.map(features, (hidden_in, query_act, key_act, value_act, ctx_grad, segment_ids))
    feat_square = lax.optimization_barrier(jnp.sum(feats * feats, axis=1))
    numerator = jnp.dot(feats.astype(jnp.bfloat16), seed_feats.T, preferred_element_type=jnp.float32)
    return numerator * lax.rsqrt(feat_square / K + EPS)[:, None] * K ** (-0.5)
```

```python
import functools
import math

import jax
import jax.numpy as jnp
from jax import lax
from jax.experimental import pallas as pl
from jax.experimental.pallas import tpu as pltpu
from jax.sharding import PartitionSpec as P

H = 64
KVH = 8
DH = 128
R = 128
K = 8192
PB = 128
NT = 8
KB = K // PB
REACH = 256

EPS = 1e-06
BF = jnp.bfloat16
F32 = jnp.float32
NEG = -1e30


def dot(a, b):
    return jnp.dot(a, b, preferred_element_type=F32)


def dot_nt(a, b):
    return lax.dot_general(a, b, (((1,), (1,)), ((), ())), preferred_element_type=F32)


def build_mask(seg_ref, mask_ref, b):
    seq = mask_ref.shape[0]
    row = seg_ref[b : b + 1, :].astype(F32)
    column = jnp.broadcast_to(row, (128, seq)).T[:, :1]
    for lo in range(0, seq, REACH):
        shape = (seq, REACH)
        key_pos = lax.broadcasted_iota(jnp.int32, shape, 0)
        query_pos = lax.broadcasted_iota(jnp.int32, shape, 1) + lo
        same = column == row[:, lo : lo + REACH]
        allowed = jnp.logical_and(key_pos <= query_pos, same)
        mask_ref[:, lo : lo + REACH] = jnp.where(allowed, 0.0, NEG)


def attend(b, g, repeats, q_v, c_v, k_v, v_v, mask, vsum, dq_t, vg):
    seq = mask.shape[0]
    kv_cols = slice(g * DH, (g + 1) * DH)
    keys = k_v[b, :, kv_cols]
    vals = v_v[b, :, kv_cols]
    keys_t = keys.T
    scale = 1.0 / math.sqrt(DH)
    vsum[...] = jnp.zeros_like(vsum)

    def head(h, carry):
        cols = pl.ds(pl.multiple_of((g * repeats + h) * DH, DH), DH)
        for lo in range(0, seq, REACH):
            first = max(lo - REACH, 0)
            rows = slice(first, lo + REACH)
            quer = q_v[b, lo : lo + REACH, cols]
            cot = c_v[b, lo : lo + REACH, cols]
            logit = dot_nt(keys[rows], quer) + mask[rows, lo : lo + REACH]
            prob_grad = dot_nt(vals[rows], cot)
            top = jnp.max(logit, axis=0, keepdims=True)
            terms = jnp.exp2((logit - top) * (scale * math.log2(math.e)))
            inv = 1.0 / jnp.sum(terms, axis=0, keepdims=True)
            probs = terms * inv
            delta = jnp.sum(probs * prob_grad, axis=0, keepdims=True)
            logit_grad = (probs * (prob_grad - delta)).astype(BF)
            vsum[rows, :] += dot(probs.astype(BF), cot)
            dq = dot(keys_t[:, rows], logit_grad) * scale
            dq_t[b, cols, lo : lo + REACH] = dq.astype(BF)
        return carry

    lax.fori_loop(0, repeats, head, 0)
    vg[b, :, kv_cols] = vsum[...].astype(BF)


def back_partial(b, kv_count, upq, upv, dq_t, vg):
    back_q = dot(upq[...], dq_t[b])
    back_v = jnp.zeros((R, vg.shape[1]), F32)
    for g in range(kv_count):
        cols = slice(g * DH, (g + 1) * DH)
        back_v += dot_nt(upv[:, cols], vg[b, :, cols])
    return back_q, back_v


def attention_kernel(
    kv_count, repeats,
    hid, que, key, val, ctx, seg, downq, upq_h, downv, upv_h,
    dq_t, vg, low, back,
    h_v, q_v, c_v, k_v, v_v, dn, upq, upv, mask, vsum, sems,
):
    m = lax.axis_index("mp")
    heads = kv_count * repeats
    kv_first = m * heads // (H // KVH)
    kv_cols = pl.ds(pl.multiple_of(kv_first * DH, DH), kv_count * DH)
    cands = que.shape[0]
    count = [0]

    def load(src, dst):
        copy = pltpu.make_async_copy(src, dst, sems.at[count[0]])
        count[0] += 1
        copy.start()
        return copy

    kv_copies = [load(key.at[:, :, kv_cols], k_v), load(val.at[:, :, kv_cols], v_v)]
    tok = [[load(que.at[b], q_v.at[b]), load(ctx.at[b], c_v.at[b])] for b in range(cands)]
    late = [load(hid.at[b], h_v.at[b]) for b in range(cands)]
    late += [load(downq, dn.at[:, :R]), load(downv, dn.at[:, R:]), load(upq_h, upq)]
    late += [load(upv_h.at[:, kv_cols], upv)]
    for copy in kv_copies:
        copy.wait()
    for b in range(cands):
        build_mask(seg, mask, b)
        for copy in tok[b]:
            copy.wait()
        for g in range(kv_count):
            attend(b, g, repeats, q_v, c_v, k_v, v_v, mask, vsum, dq_t, vg)
        if b == 0:
            for copy in late:
                copy.wait()
            for c in range(cands):
                low[c] = dot(h_v[c], dn[...]).astype(BF)
        back_q, back_v = back_partial(b, kv_count, upq, upv, dq_t, vg)
        back[b, :R, :] = back_q.astype(BF)
        back[b, R:, :] = back_v.astype(BF)


CHUNK = 256


def bucket_add(sums, ids, grads, transposed):
    buckets = sums.shape[0]
    spots = lax.broadcasted_iota(jnp.int32, (buckets, ids.shape[1]), 0)
    hot = jnp.where(spots == ids, 1.0, 0.0).astype(BF)
    sums[...] += (dot_nt if transposed else dot)(hot, grads)


def add_upq(sums, ids, dq_t, low):
    cands, width = dq_t.shape[0], dq_t.shape[1]
    chunk = min(CHUNK, width)

    def step(i, carry):
        rows = pl.ds(pl.multiple_of(i * chunk, chunk), chunk)
        grads = [dot(dq_t[b, rows, :], low[b, :, :R]) for b in range(cands)]
        bucket_add(sums, ids[2:3, rows], jnp.concatenate(grads, axis=1).astype(BF), False)
        return carry

    lax.fori_loop(0, width // chunk, step, 0)


def add_upv(sums, ids, vg, low):
    cands, width = vg.shape[0], vg.shape[2]
    grads = [dot(vg[b].T, low[b, :, R:]) for b in range(cands)]
    bucket_add(sums, ids[...], jnp.concatenate(grads, axis=1).astype(BF), False)


def add_down(sums, ids, h_v, back):
    cands, width = h_v.shape[0], h_v.shape[2]
    chunk = min(CHUNK, width)

    def step(i, carry):
        cols = pl.ds(pl.multiple_of(i * chunk, chunk), chunk)
        grads = [dot(back[b], h_v[b, :, cols]).astype(BF) for b in range(cands)]
        for j in range(2):
            part = jnp.concatenate([grad[j * R : (j + 1) * R] for grad in grads], axis=0)
            bucket_add(sums, ids[j : j + 1, cols], part, True)
        return carry

    lax.fori_loop(0, width // chunk, step, 0)


def project(sums, bank, b):
    total = jnp.zeros((KB, PB), F32)
    for t in range(NT):
        part = sums[t * KB : (t + 1) * KB, b * R : (b + 1) * R].astype(BF)
        total += dot(part, bank[t])
    return total


def feature_kernel(hid, dq_t, vg, low, back, ids, ids_v, bank, feats, sums):
    sums[...] = jnp.zeros_like(sums)
    add_upq(sums, ids, dq_t, low)
    add_upv(sums, ids_v, vg, low)
    add_down(sums, ids, hid, back)
    for b in range(hid.shape[0]):
        feats[b] = project(sums, bank, b).astype(BF)


ANY = pl.BlockSpec(memory_space=pl.ANY)
VMEM = pl.BlockSpec(memory_space=pltpu.VMEM)


def local(
    hidden_in, query_act, key_act, value_act, ctx_grad, segment_ids,
    down_query, up_query, down_value, up_value,
    block_rows, tile_rows, block_value, tile_value, tile_bank, seed_feats,
):
    cands, seq, width = query_act.shape
    heads = width // DH
    kv_count = max(heads // (H // KVH), 1)
    repeats = heads // kv_count
    kvw = kv_count * DH
    kv_first = lax.axis_index("mp") * heads // (H // KVH)
    seeds_all = lax.all_gather(seed_feats, "dp", axis=0, tiled=True)
    ids = tile_rows * KB + block_rows
    ids_v = lax.dynamic_slice_in_dim(tile_value * KB + block_value, kv_first * DH, kvw, 0)[None]
    dq_t, vg, low, back = pl.pallas_call(
        functools.partial(attention_kernel, kv_count, repeats),
        out_shape=(
            jax.ShapeDtypeStruct((cands, width, seq), BF),
            jax.ShapeDtypeStruct((cands, seq, kvw), BF),
            jax.ShapeDtypeStruct((cands, seq, 2 * R), BF),
            jax.ShapeDtypeStruct((cands, 2 * R, seq), BF),
        ),
        in_specs=[ANY] * 5 + [VMEM] + [ANY] * 4,
        out_specs=(VMEM,) * 4,
        scratch_shapes=[
            pltpu.VMEM((cands, seq, width), BF),
            pltpu.VMEM((cands, seq, width), BF),
            pltpu.VMEM((cands, seq, width), BF),
            pltpu.VMEM((cands, seq, kvw), BF),
            pltpu.VMEM((cands, seq, kvw), BF),
            pltpu.VMEM((width, 2 * R), BF),
            pltpu.VMEM((R, width), BF),
            pltpu.VMEM((R, kvw), BF),
            pltpu.VMEM((seq, seq), F32),
            pltpu.VMEM((seq, DH), F32),
            pltpu.SemaphoreType.DMA((6 + 3 * cands,)),
        ],
        compiler_params=pltpu.CompilerParams(vmem_limit_bytes=56 << 20),
        cost_estimate=pl.CostEstimate(
            flops=cands * heads * seq * seq * DH * 8, bytes_accessed=16 << 20,
            transcendentals=cands * heads * seq * seq,
        ),
        name="attention",
    )(hidden_in, query_act, key_act, value_act, ctx_grad, segment_ids,
      down_query, up_query, down_value, up_value)
    low, back = lax.psum((low, back), "mp")
    feats = pl.pallas_call(
        feature_kernel,
        out_shape=jax.ShapeDtypeStruct((cands, KB, PB), BF),
        in_specs=[VMEM] * 8,
        out_specs=VMEM,
        scratch_shapes=[pltpu.VMEM((KB * NT, cands * R), F32)],
        compiler_params=pltpu.CompilerParams(vmem_limit_bytes=56 << 20),
        cost_estimate=pl.CostEstimate(
            flops=cands * seq * width * R * 8, bytes_accessed=8 << 20, transcendentals=0
        ),
        name="features",
    )(hidden_in, dq_t, vg, low, back, ids, ids_v, tile_bank)
    feat_slice = lax.psum_scatter(
        feats.reshape(cands, K), "mp", scatter_dimension=1, tiled=True
    ).astype(F32)
    feat_square = jnp.sum(feat_slice * feat_slice, axis=1)
    partial_value = jnp.einsum(
        "bk,sk->bs", feat_slice.astype(BF), seeds_all, preferred_element_type=F32
    )
    total_square = lax.psum(feat_square, "mp")
    numerator = lax.psum_scatter(partial_value, "mp", scatter_dimension=1, tiled=True)
    return numerator * lax.rsqrt(total_square / K + EPS)[:, None] * K ** (-0.5)


def solution(mesh):
    return jax.shard_map(
        local,
        mesh=mesh,
        in_specs=(
            P("dp", None, "mp"),
            P("dp", None, "mp"),
            P("dp", None, None),
            P("dp", None, None),
            P("dp", None, "mp"),
            P("dp", None),
            P("mp", None),
            P(None, "mp"),
            P("mp", None),
            P(),
            P(None, "mp"),
            P(None, "mp"),
            P(),
            P(),
            P(),
            P("dp", "mp"),
        ),
        out_specs=P("dp", "mp"),
        check_vma=False,
    )
```

```python
import functools
import math

import jax
import jax.numpy as jnp
from jax import lax
from jax.experimental import pallas as pl
from jax.experimental.pallas import tpu as pltpu
from jax.sharding import PartitionSpec as P

H = 64
KVH = 8
DH = 128
R = 128
K = 8192
PB = 128
NT = 8
KB = K // PB
REACH = 256

EPS = 1e-06
BF = jnp.bfloat16
F32 = jnp.float32
NEG = -1e30


def dot(a, b):
    return jnp.dot(a, b, preferred_element_type=F32)


def dot_nt(a, b):
    return lax.dot_general(a, b, (((1,), (1,)), ((), ())), preferred_element_type=F32)


def build_mask(seg_ref, mask_ref, b):
    seq = mask_ref.shape[0]
    row = seg_ref[b : b + 1, :].astype(F32)
    column = jnp.broadcast_to(row, (128, seq)).T[:, :1]
    for lo in range(0, seq, REACH):
        shape = (seq, REACH)
        key_pos = lax.broadcasted_iota(jnp.int32, shape, 0)
        query_pos = lax.broadcasted_iota(jnp.int32, shape, 1) + lo
        same = column == row[:, lo : lo + REACH]
        allowed = jnp.logical_and(key_pos <= query_pos, same)
        mask_ref[:, lo : lo + REACH] = jnp.where(allowed, 0.0, NEG)


def attend(b, g, repeats, q_v, c_v, k_v, v_v, mask, vsum, dq_t, vg):
    seq = mask.shape[0]
    kv_cols = slice(g * DH, (g + 1) * DH)
    keys = k_v[b, :, kv_cols]
    vals = v_v[b, :, kv_cols]
    keys_t = keys.T
    scale = 1.0 / math.sqrt(DH)
    vsum[...] = jnp.zeros_like(vsum)

    def head(h, carry):
        cols = pl.ds(pl.multiple_of((g * repeats + h) * DH, DH), DH)
        for lo in range(0, seq, REACH):
            first = max(lo - REACH, 0)
            rows = slice(first, lo + REACH)
            quer = q_v[b, lo : lo + REACH, cols]
            cot = c_v[b, lo : lo + REACH, cols]
            logit = dot_nt(keys[rows], quer) + mask[rows, lo : lo + REACH]
            prob_grad = dot_nt(vals[rows], cot)
            top = jnp.max(logit, axis=0, keepdims=True)
            terms = jnp.exp2((logit - top) * (scale * math.log2(math.e)))
            inv = 1.0 / jnp.sum(terms, axis=0, keepdims=True)
            probs = terms * inv
            delta = jnp.sum(probs * prob_grad, axis=0, keepdims=True)
            logit_grad = (probs * (prob_grad - delta)).astype(BF)
            vsum[rows, :] += dot(probs.astype(BF), cot)
            dq = dot(keys_t[:, rows], logit_grad) * scale
            dq_t[b, cols, lo : lo + REACH] = dq.astype(BF)
        return carry

    lax.fori_loop(0, repeats, head, 0)
    vg[b, :, kv_cols] = vsum[...].astype(BF)


def back_partial(b, kv_count, upq, upv, dq_t, vg):
    back_q = dot(upq[...], dq_t[b])
    back_v = jnp.zeros((R, vg.shape[1]), F32)
    for g in range(kv_count):
        cols = slice(g * DH, (g + 1) * DH)
        back_v += dot_nt(upv[:, cols], vg[b, :, cols])
    return back_q, back_v


MESH = pl.DeviceIdType.MESH


def meet(n):
    barrier = pltpu.get_barrier_semaphore()
    me = lax.axis_index("mp")
    for k in range(1, n):
        peer = (lax.axis_index("dp"), lax.rem(me + k, n))
        pl.semaphore_signal(barrier, inc=1, device_id=peer, device_id_type=MESH)
    pl.semaphore_wait(barrier, n - 1)


def spread(n, source, target, send, recv):
    me = lax.axis_index("mp")
    copies = []
    for k in range(1, n):
        peer = lax.rem(me + k, n)
        copy = pltpu.make_async_remote_copy(
            src_ref=source(peer),
            dst_ref=target(k),
            send_sem=send.at[k - 1],
            recv_sem=recv.at[k - 1],
            device_id=(lax.axis_index("dp"), peer),
            device_id_type=MESH,
        )
        copy.start()
        copies.append(copy)
    return copies


def finish(copies):
    for copy in copies:
        copy.wait()


class Reduce:
    def __init__(self, n, part, slots, full, sems):
        self.n, self.part, self.slots, self.full, self.sems = n, part, slots, full, sems

    def scatter(self):
        self.first = spread(
            self.n, lambda peer: self.part.at[peer], lambda k: self.slots.at[k - 1],
            self.sems.at[0], self.sems.at[1],
        )

    def gather(self):
        finish(self.first)
        me = lax.axis_index("mp")
        total = self.part[me].astype(F32)
        for k in range(1, self.n):
            total += self.slots[k - 1].astype(F32)
        self.full[me] = total.astype(BF)
        self.second = spread(
            self.n, lambda peer: self.full.at[me], lambda k: self.full.at[me],
            self.sems.at[2], self.sems.at[3],
        )

    def done(self):
        finish(self.second)


def main_kernel(
    n, kv_count, repeats,
    hid, que, key, val, ctx, seg, downq, upq_h, downv, upv_h, ids, ids_v, bank,
    feats,
    h_v, q_v, c_v, k_v, v_v, dn, upq, upv, mask, vsum, dq_t, vg, sums, grads0,
    low_part, low_slots, low_full, back_part, back_slots, back_full, sems, links,
):
    m = lax.axis_index("mp")
    heads = kv_count * repeats
    kv_first = m * heads // (H // KVH)
    kv_cols = pl.ds(pl.multiple_of(kv_first * DH, DH), kv_count * DH)
    cands, seq, width = que.shape
    count = [0]

    def load(src, dst):
        copy = pltpu.make_async_copy(src, dst, sems.at[count[0]])
        count[0] += 1
        copy.start()
        return copy

    early = [load(downq, dn.at[:, :R]), load(downv, dn.at[:, R:])]
    early += [load(hid.at[b], h_v.at[b]) for b in range(cands)]
    kv_copies = [load(key.at[:, :, kv_cols], k_v), load(val.at[:, :, kv_cols], v_v)]
    tok = [[load(que.at[b], q_v.at[b]), load(ctx.at[b], c_v.at[b])] for b in range(cands)]
    late = [load(upq_h, upq), load(upv_h.at[:, kv_cols], upv)]

    build_mask(seg, mask, 0)
    finish(early)
    for c in range(cands):
        low = dot(h_v[c], dn[...]).astype(BF)
        low_part[:, c] = low.reshape(n, seq // n, 2 * R)
    meet(n)
    low_sum = Reduce(n, low_part, low_slots, low_full, links.at[0])
    low_sum.scatter()
    finish(kv_copies)
    pending = low_sum
    for b in range(cands):
        if b:
            build_mask(seg, mask, b)
        finish(tok[b])
        for g in range(kv_count):
            attend(b, g, repeats, q_v, c_v, k_v, v_v, mask, vsum, dq_t, vg)
            if g == 0:
                pending.gather()
        if b == 0:
            finish(late)
        back_q, back_v = back_partial(b, kv_count, upq, upv, dq_t, vg)
        back = jnp.concatenate([back_q, back_v], axis=0).astype(BF)
        pending.done()
        back_part[b] = back.reshape(n, 2 * R // n, seq)
        pending = Reduce(
            n, back_part.at[b], back_slots.at[b], back_full.at[b], links.at[b + 1]
        )
        pending.scatter()
    low = [low_full[:, b].reshape(seq, 2 * R) for b in range(cands)]
    sums[...] = jnp.zeros_like(sums)
    add_upq(sums, ids, dq_t, low)
    pending.gather()
    add_upv(sums, ids_v, vg, low)
    for b in range(cands - 1):
        whole = back_full[b].reshape(2 * R, seq)
        for lo in range(0, width, 512):
            cols = slice(lo, lo + 512)
            grads0[b, :, cols] = dot(whole, h_v[b, :, cols]).astype(BF)
    pending.done()
    add_down(sums, ids, h_v, grads0, back_full[cands - 1].reshape(2 * R, seq))
    rows = KB // n
    for b in range(cands):
        feats[:, b] = project(sums, bank, b).reshape(n, rows, PB)


def tail_kernel(n, feats, seeds, out, slots, pack, slots2, links):
    me = lax.axis_index("mp")
    cands, rows = feats.shape[1], feats.shape[2]
    outs = out.shape[1]
    meet(n)
    first = spread(n, lambda peer: feats.at[peer], lambda k: slots.at[k - 1], links.at[0], links.at[1])
    finish(first)
    total = feats[me]
    for k in range(1, n):
        total += slots[k - 1]
    flat = jnp.concatenate(
        [
            jnp.concatenate([total[b, i : i + 1] for i in range(rows)], axis=1)
            for b in range(cands)
        ],
        axis=0,
    )
    square = jnp.sum(flat * flat, axis=1, keepdims=True)
    number = dot_nt(flat.astype(BF), seeds[...])
    for j in range(n):
        pack[j, :, :outs] = number[:, j * outs : (j + 1) * outs]
        pack[j, :, outs:] = jnp.broadcast_to(square, (cands, outs))
    second = spread(n, lambda peer: pack.at[peer], lambda k: slots2.at[k - 1], links.at[2], links.at[3])
    finish(second)
    both = pack[me]
    for k in range(1, n):
        both += slots2[k - 1]
    out[...] = both[:, :outs] * lax.rsqrt(both[:, outs:] / K + EPS) * K ** (-0.5)


CHUNK = 256


def bucket_add(sums, ids, grads, transposed):
    buckets = sums.shape[0]
    spots = lax.broadcasted_iota(jnp.int32, (buckets, ids.shape[1]), 0)
    hot = jnp.where(spots == ids, 1.0, 0.0).astype(BF)
    sums[...] += (dot_nt if transposed else dot)(hot, grads)


def add_upq(sums, ids, dq_t, low):
    cands, width = dq_t.shape[0], dq_t.shape[1]
    chunk = min(CHUNK, width)

    def step(i, carry):
        rows = pl.ds(pl.multiple_of(i * chunk, chunk), chunk)
        grads = [dot(dq_t[b, rows, :], low[b][:, :R]) for b in range(cands)]
        bucket_add(sums, ids[2:3, rows], jnp.concatenate(grads, axis=1).astype(BF), False)
        return carry

    lax.fori_loop(0, width // chunk, step, 0)


def add_upv(sums, ids, vg, low):
    cands, width = vg.shape[0], vg.shape[2]
    grads = [dot(vg[b].T, low[b][:, R:]) for b in range(cands)]
    bucket_add(sums, ids[...], jnp.concatenate(grads, axis=1).astype(BF), False)


def add_down(sums, ids, h_v, grads0, back):
    cands, width = h_v.shape[0], h_v.shape[2]
    chunk = min(CHUNK, width)

    def step(i, carry):
        cols = pl.ds(pl.multiple_of(i * chunk, chunk), chunk)
        grads = [grads0[b, :, cols] for b in range(cands - 1)]
        grads.append(dot(back, h_v[cands - 1, :, cols]).astype(BF))
        for j in range(2):
            part = jnp.concatenate([grad[j * R : (j + 1) * R] for grad in grads], axis=0)
            bucket_add(sums, ids[j : j + 1, cols], part, True)
        return carry

    lax.fori_loop(0, width // chunk, step, 0)


def project(sums, bank, b):
    total = jnp.zeros((KB, PB), F32)
    for t in range(NT):
        part = sums[t * KB : (t + 1) * KB, b * R : (b + 1) * R].astype(BF)
        total += dot(part, bank[t])
    return total


ANY = pl.BlockSpec(memory_space=pl.ANY)
VMEM = pl.BlockSpec(memory_space=pltpu.VMEM)


def local(
    hidden_in, query_act, key_act, value_act, ctx_grad, segment_ids,
    down_query, up_query, down_value, up_value,
    block_rows, tile_rows, block_value, tile_value, tile_bank, seed_feats,
):
    cands, seq, width = query_act.shape
    heads = width // DH
    kv_count = max(heads // (H // KVH), 1)
    repeats = heads // kv_count
    kvw = kv_count * DH
    kv_first = lax.axis_index("mp") * heads // (H // KVH)
    seeds_all = lax.all_gather(seed_feats, "dp", axis=0, tiled=True)
    ids = tile_rows * KB + block_rows
    ids_v = lax.dynamic_slice_in_dim(tile_value * KB + block_value, kv_first * DH, kvw, 0)[None]
    n = lax.axis_size("mp")
    hop = [pltpu.VMEM((n, cands, seq // n, 2 * R), BF), pltpu.VMEM((n - 1, cands, seq // n, 2 * R), BF)]
    fold = (2 * R // n, seq)
    feats = pl.pallas_call(
        functools.partial(main_kernel, n, kv_count, repeats),
        out_shape=jax.ShapeDtypeStruct((n, cands, KB // n, PB), F32),
        in_specs=[ANY] * 5 + [VMEM] + [ANY] * 4 + [VMEM] * 3,
        out_specs=VMEM,
        scratch_shapes=[
            pltpu.VMEM((cands, seq, width), BF),
            pltpu.VMEM((cands, seq, width), BF),
            pltpu.VMEM((cands, seq, width), BF),
            pltpu.VMEM((cands, seq, kvw), BF),
            pltpu.VMEM((cands, seq, kvw), BF),
            pltpu.VMEM((width, 2 * R), BF),
            pltpu.VMEM((R, width), BF),
            pltpu.VMEM((R, kvw), BF),
            pltpu.VMEM((seq, seq), F32),
            pltpu.VMEM((seq, DH), F32),
            pltpu.VMEM((cands, width, seq), BF),
            pltpu.VMEM((cands, seq, kvw), BF),
            pltpu.VMEM((KB * NT, cands * R), F32),
            pltpu.VMEM((max(cands - 1, 1), 2 * R, width), BF),
            hop[0], hop[1], hop[0],
            pltpu.VMEM((cands, n) + fold, BF),
            pltpu.VMEM((cands, n - 1) + fold, BF),
            pltpu.VMEM((cands, n) + fold, BF),
            pltpu.SemaphoreType.DMA((6 + 3 * cands,)),
            pltpu.SemaphoreType.DMA((cands + 1, 4, n - 1)),
        ],
        compiler_params=pltpu.CompilerParams(
            vmem_limit_bytes=56 << 20, collective_id=0, has_side_effects=True
        ),
        cost_estimate=pl.CostEstimate(
            flops=cands * heads * seq * seq * DH * 12, bytes_accessed=16 << 20,
            transcendentals=cands * heads * seq * seq,
        ),
        name="gradient_features",
    )(hidden_in, query_act, key_act, value_act, ctx_grad, segment_ids,
      down_query, up_query, down_value, up_value, ids, ids_v, tile_bank)
    outs = seeds_all.shape[0] // n
    return pl.pallas_call(
        functools.partial(tail_kernel, n),
        out_shape=jax.ShapeDtypeStruct((cands, outs), F32),
        in_specs=[VMEM] * 2,
        out_specs=VMEM,
        scratch_shapes=[
            pltpu.VMEM((n - 1, cands, KB // n, PB), F32),
            pltpu.VMEM((n, cands, 2 * outs), F32),
            pltpu.VMEM((n - 1, cands, 2 * outs), F32),
            pltpu.SemaphoreType.DMA((4, n - 1)),
        ],
        compiler_params=pltpu.CompilerParams(collective_id=1, has_side_effects=True),
        name="seed_scores",
    )(feats, seeds_all)


def solution(mesh):
    return jax.shard_map(
        local,
        mesh=mesh,
        in_specs=(
            P("dp", None, "mp"),
            P("dp", None, "mp"),
            P("dp", None, None),
            P("dp", None, None),
            P("dp", None, "mp"),
            P("dp", None),
            P("mp", None),
            P(None, "mp"),
            P("mp", None),
            P(),
            P(None, "mp"),
            P(None, "mp"),
            P(),
            P(),
            P(),
            P("dp", "mp"),
        ),
        out_specs=P("dp", "mp"),
        check_vma=False,
    )
```

```python
import functools
import math

import jax
import jax.numpy as jnp
from jax import lax
from jax.experimental import pallas as pl
from jax.experimental.pallas import tpu as pltpu
from jax.sharding import PartitionSpec as P

H = 64
KVH = 8
DH = 128
R = 128
K = 8192
PB = 128
NT = 8
KB = K // PB
REACH = 256

EPS = 1e-06
BF = jnp.bfloat16
F32 = jnp.float32
NEG = -1e30


def dot(a, b):
    return jnp.dot(a, b, preferred_element_type=F32)


def dot_nt(a, b):
    return lax.dot_general(a, b, (((1,), (1,)), ((), ())), preferred_element_type=F32)


def build_mask(seg_ref, mask_ref, b):
    seq = mask_ref.shape[0]
    row = seg_ref[b : b + 1, :].astype(F32)
    column = jnp.broadcast_to(row, (128, seq)).T[:, :1]
    for lo in range(0, seq, REACH):
        shape = (seq, REACH)
        key_pos = lax.broadcasted_iota(jnp.int32, shape, 0)
        query_pos = lax.broadcasted_iota(jnp.int32, shape, 1) + lo
        same = column == row[:, lo : lo + REACH]
        allowed = jnp.logical_and(key_pos <= query_pos, same)
        mask_ref[:, lo : lo + REACH] = jnp.where(allowed, 0.0, NEG)


UNROLL = 4


def attend(b, g, repeats, q_v, c_v, k_v, v_v, mask, vsum, dq_t, vg):
    seq = mask.shape[0]
    kv_cols = slice(g * DH, (g + 1) * DH)
    keys = k_v[b, :, kv_cols]
    vals = v_v[b, :, kv_cols]
    keys_t = keys.T
    scale = 1.0 / math.sqrt(DH)
    vsum[...] = jnp.zeros_like(vsum)

    units = [(j, lo) for j in range(UNROLL) for lo in range(0, seq, REACH)]

    def heads(i, carry):
        cols = [
            pl.ds(pl.multiple_of((g * repeats + i * UNROLL + j) * DH, DH), DH)
            for j in range(UNROLL)
        ]

        def span(lo):
            return slice(max(lo - REACH, 0), lo + REACH)

        def products(j, lo):
            quer = q_v[b, lo : lo + REACH, cols[j]]
            cot = c_v[b, lo : lo + REACH, cols[j]]
            return dot_nt(keys[span(lo)], quer), dot_nt(vals[span(lo)], cot)

        def soft(lo, logits, prob_grads):
            first, last = span(lo).start, span(lo).stop
            probs, grads = [], []
            for at in range(lo, lo + REACH, DH):
                low, high = max(at - REACH, 0), at + DH
                rows, lanes = slice(low - first, high - first), slice(at - lo, at - lo + DH)
                logit = logits[rows, lanes] + mask[low:high, at : at + DH]
                prob_grad = prob_grads[rows, lanes]
                top = jnp.max(logit, axis=0, keepdims=True)
                terms = jnp.exp2((logit - top) * (scale * math.log2(math.e)))
                prob = terms * (1.0 / jnp.sum(terms, axis=0, keepdims=True))
                delta = jnp.sum(prob * prob_grad, axis=0, keepdims=True)

                def padded(block):
                    above = jnp.zeros((low - first, DH), BF)
                    below = jnp.zeros((last - high, DH), BF)
                    parts = [p for p in (above, block.astype(BF), below) if p.shape[0]]
                    return jnp.concatenate(parts, axis=0) if len(parts) > 1 else parts[0]

                probs.append(padded(prob))
                grads.append(padded(prob * (prob_grad - delta)))
            return jnp.concatenate(probs, axis=1), jnp.concatenate(grads, axis=1)

        held = {}
        ready = products(*units[0])
        for at, (j, lo) in enumerate(units):
            logits, prob_grads = ready
            if at + 1 < len(units):
                ready = products(*units[at + 1])
            probs, grads = soft(lo, logits, prob_grads)
            held[j, lo] = probs
            dq = dot(keys_t[:, span(lo)], grads) * scale
            dq_t[b, cols[j], lo : lo + REACH] = dq.astype(BF)
        for lo in range(0, seq, REACH):
            probs = jnp.concatenate([held[j, lo] for j in range(UNROLL)], axis=1)
            cots = jnp.concatenate(
                [c_v[b, lo : lo + REACH, cols[j]] for j in range(UNROLL)], axis=0
            )
            vsum[span(lo), :] += dot(probs, cots)
        return carry

    lax.fori_loop(0, repeats // UNROLL, heads, 0)
    vg[b, :, kv_cols] = vsum[...].astype(BF)


def back_partial(b, kv_count, upq, upv, dq_t, vg):
    back_q = dot(upq[...], dq_t[b])
    back_v = jnp.zeros((R, vg.shape[1]), F32)
    for g in range(kv_count):
        cols = slice(g * DH, (g + 1) * DH)
        back_v += dot_nt(upv[:, cols], vg[b, :, cols])
    return back_q, back_v


MESH = pl.DeviceIdType.MESH


def meet(n):
    barrier = pltpu.get_barrier_semaphore()
    me = lax.axis_index("mp")
    for k in range(1, n):
        peer = (lax.axis_index("dp"), lax.rem(me + k, n))
        pl.semaphore_signal(barrier, inc=1, device_id=peer, device_id_type=MESH)
    pl.semaphore_wait(barrier, n - 1)


def spread(n, source, target, send, recv):
    me = lax.axis_index("mp")
    copies = []
    for k in range(1, n):
        peer = lax.rem(me + k, n)
        copy = pltpu.make_async_remote_copy(
            src_ref=source(peer),
            dst_ref=target(k),
            send_sem=send.at[k - 1],
            recv_sem=recv.at[k - 1],
            device_id=(lax.axis_index("dp"), peer),
            device_id_type=MESH,
        )
        copy.start()
        copies.append(copy)
    return copies


def finish(copies):
    for copy in copies:
        copy.wait()


class Reduce:
    def __init__(self, n, part, slots, full, sems):
        self.n, self.part, self.slots, self.full, self.sems = n, part, slots, full, sems

    def scatter(self):
        self.first = spread(
            self.n, lambda peer: self.part.at[peer], lambda k: self.slots.at[k - 1],
            self.sems.at[0], self.sems.at[1],
        )

    def gather(self):
        finish(self.first)
        me = lax.axis_index("mp")
        total = self.part[me].astype(F32)
        for k in range(1, self.n):
            total += self.slots[k - 1].astype(F32)
        self.full[me] = total.astype(BF)
        self.second = spread(
            self.n, lambda peer: self.full.at[me], lambda k: self.full.at[me],
            self.sems.at[2], self.sems.at[3],
        )

    def done(self):
        finish(self.second)


def main_kernel(
    n, kv_count, repeats,
    hid, que, key, val, ctx, seg, downq, upq_h, downv, upv_h,
    block, tile, block_v, tile_v, bank,
    feats,
    h_v, q_v, c_v, k_v, v_v, dn, upq, upv, mask, vsum, dq_t, vg, sums, grads0, ids_s,
    low_part, low_slots, low_full, back_part, back_slots, back_full, sems, links,
):
    m = lax.axis_index("mp")
    heads = kv_count * repeats
    kv_first = m * heads // (H // KVH)
    kv_cols = pl.ds(pl.multiple_of(kv_first * DH, DH), kv_count * DH)
    cands, seq, width = que.shape
    count = [0]

    def load(src, dst):
        copy = pltpu.make_async_copy(src, dst, sems.at[count[0]])
        count[0] += 1
        copy.start()
        return copy

    early = [load(downq, dn.at[:, :R]), load(downv, dn.at[:, R:])]
    early += [load(hid.at[b], h_v.at[b]) for b in range(cands)]
    kv_copies = [load(key.at[:, :, kv_cols], k_v), load(val.at[:, :, kv_cols], v_v)]
    tok = [[load(que.at[b], q_v.at[b]), load(ctx.at[b], c_v.at[b])] for b in range(cands)]
    late = [load(upq_h, upq), load(upv_h.at[:, kv_cols], upv)]

    build_mask(seg, mask, 0)
    finish(early[:2])
    for c in range(cands):
        early[2 + c].wait()
        low = dot(h_v[c], dn[...]).astype(BF)
        low_part[:, c] = low.reshape(n, seq // n, 2 * R)
    meet(n)
    low_sum = Reduce(n, low_part, low_slots, low_full, links.at[0])
    low_sum.scatter()
    finish(kv_copies)
    pending = low_sum
    for b in range(cands):
        if b:
            build_mask(seg, mask, b)
        finish(tok[b])
        for g in range(kv_count):
            attend(b, g, repeats, q_v, c_v, k_v, v_v, mask, vsum, dq_t, vg)
            if g == 0:
                pending.gather()
        if b == 0:
            finish(late)
        back_q, back_v = back_partial(b, kv_count, upq, upv, dq_t, vg)
        back = jnp.concatenate([back_q, back_v], axis=0).astype(BF)
        pending.done()
        back_part[b] = back.reshape(n, 2 * R // n, seq)
        pending = Reduce(
            n, back_part.at[b], back_slots.at[b], back_full.at[b], links.at[b + 1]
        )
        pending.scatter()
    low = [low_full[:, b].reshape(seq, 2 * R) for b in range(cands)]
    sums[...] = jnp.zeros_like(sums)
    ids = tile[...] * KB + block[...]
    ids_v = tile_v[:, kv_cols] * KB + block_v[:, kv_cols]
    ids_s[...] = ids
    add_upq(sums, ids_s, dq_t, low)
    pending.gather()
    add_upv(sums, ids_v, vg, low)
    for b in range(cands - 1):
        whole = back_full[b].reshape(2 * R, seq)
        for lo in range(0, width, 512):
            cols = slice(lo, lo + 512)
            grads0[b, :, cols] = dot(whole, h_v[b, :, cols]).astype(BF)
    pending.done()
    add_down(sums, ids_s, h_v, grads0, back_full[cands - 1].reshape(2 * R, seq))
    rows = KB // n
    for b in range(cands):
        feats[:, b] = project(sums, bank, b).reshape(n, rows, PB)


def tail_kernel(n, feats, seeds, out, slots, pack, slots2, links):
    me = lax.axis_index("mp")
    cands, rows = feats.shape[1], feats.shape[2]
    outs = out.shape[1]
    meet(n)
    first = spread(n, lambda peer: feats.at[peer], lambda k: slots.at[k - 1], links.at[0], links.at[1])
    finish(first)
    total = feats[me]
    for k in range(1, n):
        total += slots[k - 1]
    flat = jnp.concatenate(
        [
            jnp.concatenate([total[b, i : i + 1] for i in range(rows)], axis=1)
            for b in range(cands)
        ],
        axis=0,
    )
    square = jnp.sum(flat * flat, axis=1, keepdims=True)
    number = dot_nt(flat.astype(BF), seeds[...])
    for j in range(n):
        pack[j, :, :outs] = number[:, j * outs : (j + 1) * outs]
        pack[j, :, outs:] = jnp.broadcast_to(square, (cands, outs))
    second = spread(n, lambda peer: pack.at[peer], lambda k: slots2.at[k - 1], links.at[2], links.at[3])
    finish(second)
    both = pack[me]
    for k in range(1, n):
        both += slots2[k - 1]
    out[...] = both[:, :outs] * lax.rsqrt(both[:, outs:] / K + EPS) * K ** (-0.5)


CHUNK = 256


def bucket_add(sums, ids, grads, transposed):
    buckets = sums.shape[0]
    spots = lax.broadcasted_iota(jnp.int32, (buckets, ids.shape[1]), 0)
    hot = jnp.where(spots == ids, 1.0, 0.0).astype(BF)
    sums[...] += (dot_nt if transposed else dot)(hot, grads)


def add_upq(sums, ids, dq_t, low):
    cands, width = dq_t.shape[0], dq_t.shape[1]
    chunk = min(CHUNK, width)

    def step(i, carry):
        rows = pl.ds(pl.multiple_of(i * chunk, chunk), chunk)
        grads = [dot(dq_t[b, rows, :], low[b][:, :R]) for b in range(cands)]
        bucket_add(sums, ids[2:3, rows], jnp.concatenate(grads, axis=1).astype(BF), False)
        return carry

    lax.fori_loop(0, width // chunk, step, 0)


def add_upv(sums, ids, vg, low):
    cands, width = vg.shape[0], vg.shape[2]
    grads = [dot(vg[b].T, low[b][:, R:]) for b in range(cands)]
    bucket_add(sums, ids, jnp.concatenate(grads, axis=1).astype(BF), False)


def add_down(sums, ids, h_v, grads0, back):
    cands, width = h_v.shape[0], h_v.shape[2]
    chunk = min(CHUNK, width)

    def step(i, carry):
        cols = pl.ds(pl.multiple_of(i * chunk, chunk), chunk)
        grads = [grads0[b, :, cols] for b in range(cands - 1)]
        grads.append(dot(back, h_v[cands - 1, :, cols]).astype(BF))
        for j in range(2):
            part = jnp.concatenate([grad[j * R : (j + 1) * R] for grad in grads], axis=0)
            bucket_add(sums, ids[j : j + 1, cols], part, True)
        return carry

    lax.fori_loop(0, width // chunk, step, 0)


def project(sums, bank, b):
    total = jnp.zeros((KB, PB), F32)
    for t in range(NT):
        part = sums[t * KB : (t + 1) * KB, b * R : (b + 1) * R].astype(BF)
        total += dot(part, bank[t])
    return total


ANY = pl.BlockSpec(memory_space=pl.ANY)
VMEM = pl.BlockSpec(memory_space=pltpu.VMEM)


def local(
    hidden_in, query_act, key_act, value_act, ctx_grad, segment_ids,
    down_query, up_query, down_value, up_value,
    block_rows, tile_rows, block_value, tile_value, tile_bank, seed_feats,
):
    cands, seq, width = query_act.shape
    heads = width // DH
    kv_count = max(heads // (H // KVH), 1)
    repeats = heads // kv_count
    kvw = kv_count * DH
    seeds_all = lax.all_gather(seed_feats, "dp", axis=0, tiled=True)
    n = lax.axis_size("mp")
    hop = [pltpu.VMEM((n, cands, seq // n, 2 * R), BF), pltpu.VMEM((n - 1, cands, seq // n, 2 * R), BF)]
    fold = (2 * R // n, seq)
    feats = pl.pallas_call(
        functools.partial(main_kernel, n, kv_count, repeats),
        out_shape=jax.ShapeDtypeStruct((n, cands, KB // n, PB), F32),
        in_specs=[ANY] * 5 + [VMEM] + [ANY] * 4 + [VMEM] * 5,
        out_specs=VMEM,
        scratch_shapes=[
            pltpu.VMEM((cands, seq, width), BF),
            pltpu.VMEM((cands, seq, width), BF),
            pltpu.VMEM((cands, seq, width), BF),
            pltpu.VMEM((cands, seq, kvw), BF),
            pltpu.VMEM((cands, seq, kvw), BF),
            pltpu.VMEM((width, 2 * R), BF),
            pltpu.VMEM((R, width), BF),
            pltpu.VMEM((R, kvw), BF),
            pltpu.VMEM((seq, seq), F32),
            pltpu.VMEM((seq, DH), F32),
            pltpu.VMEM((cands, width, seq), BF),
            pltpu.VMEM((cands, seq, kvw), BF),
            pltpu.VMEM((KB * NT, cands * R), F32),
            pltpu.VMEM((max(cands - 1, 1), 2 * R, width), BF),
            pltpu.VMEM(block_rows.shape, jnp.int32),
            hop[0], hop[1], hop[0],
            pltpu.VMEM((cands, n) + fold, BF),
            pltpu.VMEM((cands, n - 1) + fold, BF),
            pltpu.VMEM((cands, n) + fold, BF),
            pltpu.SemaphoreType.DMA((6 + 3 * cands,)),
            pltpu.SemaphoreType.DMA((cands + 1, 4, n - 1)),
        ],
        compiler_params=pltpu.CompilerParams(
            vmem_limit_bytes=56 << 20, collective_id=0, has_side_effects=True
        ),
        cost_estimate=pl.CostEstimate(
            flops=cands * heads * seq * seq * DH * 12, bytes_accessed=16 << 20,
            transcendentals=cands * heads * seq * seq,
        ),
        name="gradient_features",
    )(hidden_in, query_act, key_act, value_act, ctx_grad, segment_ids,
      down_query, up_query, down_value, up_value,
      block_rows, tile_rows, block_value[None], tile_value[None], tile_bank)
    outs = seeds_all.shape[0] // n
    return pl.pallas_call(
        functools.partial(tail_kernel, n),
        out_shape=jax.ShapeDtypeStruct((cands, outs), F32),
        in_specs=[VMEM] * 2,
        out_specs=VMEM,
        scratch_shapes=[
            pltpu.VMEM((n - 1, cands, KB // n, PB), F32),
            pltpu.VMEM((n, cands, 2 * outs), F32),
            pltpu.VMEM((n - 1, cands, 2 * outs), F32),
            pltpu.SemaphoreType.DMA((4, n - 1)),
        ],
        compiler_params=pltpu.CompilerParams(collective_id=1, has_side_effects=True),
        name="seed_scores",
    )(feats, seeds_all)


def solution(mesh):
    return jax.shard_map(
        local,
        mesh=mesh,
        in_specs=(
            P("dp", None, "mp"),
            P("dp", None, "mp"),
            P("dp", None, None),
            P("dp", None, None),
            P("dp", None, "mp"),
            P("dp", None),
            P("mp", None),
            P(None, "mp"),
            P("mp", None),
            P(),
            P(None, "mp"),
            P(None, "mp"),
            P(),
            P(),
            P(),
            P("dp", "mp"),
        ),
        out_specs=P("dp", "mp"),
        check_vma=False,
    )
```

```python
import functools
import math

import jax
import jax.numpy as jnp
from jax import lax
from jax.experimental import pallas as pl
from jax.experimental.pallas import tpu as pltpu
from jax.sharding import PartitionSpec as P

H = 64
KVH = 8
DH = 128
R = 128
K = 8192
PB = 128
NT = 8
KB = K // PB
REACH = 256

EPS = 1e-06
BF = jnp.bfloat16
F32 = jnp.float32
NEG = -1e30


def dot(a, b):
    return jnp.dot(a, b, preferred_element_type=F32)


def dot_nt(a, b):
    return lax.dot_general(a, b, (((1,), (1,)), ((), ())), preferred_element_type=F32)


def build_mask(seg_ref, mask_ref, b):
    seq = mask_ref.shape[0]
    row = seg_ref[b : b + 1, :].astype(F32)
    column = jnp.broadcast_to(row, (128, seq)).T[:, :1]
    for lo in range(0, seq, REACH):
        shape = (seq, REACH)
        key_pos = lax.broadcasted_iota(jnp.int32, shape, 0)
        query_pos = lax.broadcasted_iota(jnp.int32, shape, 1) + lo
        same = column == row[:, lo : lo + REACH]
        allowed = jnp.logical_and(key_pos <= query_pos, same)
        mask_ref[:, lo : lo + REACH] = jnp.where(allowed, 0.0, NEG)


UNROLL = 4


def attend(b, g, repeats, q_v, c_v, k_v, v_v, mask, vsum, dq_t, vg):
    seq = mask.shape[0]
    kv_cols = slice(g * DH, (g + 1) * DH)
    keys = k_v[b, :, kv_cols]
    vals = v_v[b, :, kv_cols]
    keys_t = keys.T
    scale = 1.0 / math.sqrt(DH)
    vsum[...] = jnp.zeros_like(vsum)

    units = [(j, lo) for j in range(UNROLL) for lo in range(0, seq, REACH)]

    def heads(i, carry):
        cols = [
            pl.ds(pl.multiple_of((g * repeats + i * UNROLL + j) * DH, DH), DH)
            for j in range(UNROLL)
        ]

        def span(lo):
            return slice(max(lo - REACH, 0), lo + REACH)

        def products(j, lo):
            quer = q_v[b, lo : lo + REACH, cols[j]]
            cot = c_v[b, lo : lo + REACH, cols[j]]
            return dot_nt(keys[span(lo)], quer), dot_nt(vals[span(lo)], cot)

        def soft(lo, logits, prob_grads):
            first, last = span(lo).start, span(lo).stop
            probs, grads = [], []
            for at in range(lo, lo + REACH, DH):
                low, high = max(at - REACH, 0), at + DH
                rows, lanes = slice(low - first, high - first), slice(at - lo, at - lo + DH)
                logit = logits[rows, lanes] + mask[low:high, at : at + DH]
                prob_grad = prob_grads[rows, lanes]
                top = jnp.max(logit, axis=0, keepdims=True)
                terms = jnp.exp2((logit - top) * (scale * math.log2(math.e)))
                prob = terms * (1.0 / jnp.sum(terms, axis=0, keepdims=True))
                delta = jnp.sum(prob * prob_grad, axis=0, keepdims=True)

                def padded(block):
                    above = jnp.zeros((low - first, DH), BF)
                    below = jnp.zeros((last - high, DH), BF)
                    parts = [p for p in (above, block.astype(BF), below) if p.shape[0]]
                    return jnp.concatenate(parts, axis=0) if len(parts) > 1 else parts[0]

                probs.append(padded(prob))
                grads.append(padded(prob * (prob_grad - delta)))
            return jnp.concatenate(probs, axis=1), jnp.concatenate(grads, axis=1)

        held = {}
        ready = products(*units[0])
        for at, (j, lo) in enumerate(units):
            logits, prob_grads = ready
            if at + 1 < len(units):
                ready = products(*units[at + 1])
            probs, grads = soft(lo, logits, prob_grads)
            held[j, lo] = probs
            dq = dot(keys_t[:, span(lo)], grads) * scale
            dq_t[b, cols[j], lo : lo + REACH] = dq.astype(BF)
        for lo in range(0, seq, REACH):
            probs = jnp.concatenate([held[j, lo] for j in range(UNROLL)], axis=1)
            cots = jnp.concatenate(
                [c_v[b, lo : lo + REACH, cols[j]] for j in range(UNROLL)], axis=0
            )
            vsum[span(lo), :] += dot(probs, cots)
        return carry

    lax.fori_loop(0, repeats // UNROLL, heads, 0)
    vg[b, :, kv_cols] = vsum[...].astype(BF)


def back_partial(b, kv_count, upq, upv, dq_t, vg):
    back_q = dot(upq[...], dq_t[b])
    back_v = jnp.zeros((R, vg.shape[1]), F32)
    for g in range(kv_count):
        cols = slice(g * DH, (g + 1) * DH)
        back_v += dot_nt(upv[:, cols], vg[b, :, cols])
    return back_q, back_v


MESH = pl.DeviceIdType.MESH


def device(axis, peer):
    if axis == "dp":
        return (peer, lax.axis_index("mp"))
    return (lax.axis_index("dp"), peer)


def meet(sizes):
    barrier = pltpu.get_barrier_semaphore()
    for axis, n in sizes:
        me = lax.axis_index(axis)
        for k in range(1, n):
            peer = device(axis, lax.rem(me + k, n))
            pl.semaphore_signal(barrier, inc=1, device_id=peer, device_id_type=MESH)
    pl.semaphore_wait(barrier, sum(n - 1 for _, n in sizes))


def spread(axis, n, source, target, send, recv):
    me = lax.axis_index(axis)
    copies = []
    for k in range(1, n):
        peer = lax.rem(me + k, n)
        copy = pltpu.make_async_remote_copy(
            src_ref=source(peer),
            dst_ref=target(k),
            send_sem=send.at[k - 1],
            recv_sem=recv.at[k - 1],
            device_id=device(axis, peer),
            device_id_type=MESH,
        )
        copy.start()
        copies.append(copy)
    return copies


def finish(copies):
    for copy in copies:
        copy.wait()


class Reduce:
    def __init__(self, n, part, slots, full, sems):
        self.n, self.part, self.slots, self.full, self.sems = n, part, slots, full, sems

    def scatter(self):
        self.first = spread(
            "mp", self.n, lambda peer: self.part.at[peer], lambda k: self.slots.at[k - 1],
            self.sems.at[0], self.sems.at[1],
        )

    def gather(self):
        finish(self.first)
        me = lax.axis_index("mp")
        total = self.part[me].astype(F32)
        for k in range(1, self.n):
            total += self.slots[k - 1].astype(F32)
        self.full[me] = total.astype(BF)
        self.second = spread(
            "mp", self.n, lambda peer: self.full.at[me], lambda k: self.full.at[me],
            self.sems.at[2], self.sems.at[3],
        )

    def done(self):
        finish(self.second)


def main_kernel(
    n, dp, kv_count, repeats,
    hid, que, key, val, ctx, seg, downq, upq_h, downv, upv_h,
    block, tile, block_v, tile_v, bank, seeds,
    out,
    h_v, q_v, c_v, k_v, v_v, dn, upq, upv, mask, vsum, dq_t, vg, sums, grads0, ids_s,
    low_part, low_slots, low_full, back_part, back_slots, back_full,
    feats, feat_slots, pack, pack_slots, seeds_all, sems, links, seed_links,
):
    m = lax.axis_index("mp")
    heads = kv_count * repeats
    kv_first = m * heads // (H // KVH)
    kv_cols = pl.ds(pl.multiple_of(kv_first * DH, DH), kv_count * DH)
    cands, seq, width = que.shape
    count = [0]

    def load(src, dst):
        copy = pltpu.make_async_copy(src, dst, sems.at[count[0]])
        count[0] += 1
        copy.start()
        return copy

    early = [load(downq, dn.at[:, :R]), load(downv, dn.at[:, R:])]
    early += [load(hid.at[b], h_v.at[b]) for b in range(cands)]
    kv_copies = [load(key.at[:, :, kv_cols], k_v), load(val.at[:, :, kv_cols], v_v)]
    tok = [[load(que.at[b], q_v.at[b]), load(ctx.at[b], c_v.at[b])] for b in range(cands)]
    late = [load(upq_h, upq), load(upv_h.at[:, kv_cols], upv)]

    build_mask(seg, mask, 0)
    spot = lax.axis_index("dp")
    seeds_all[spot] = seeds[...]
    meet((("mp", n), ("dp", dp)))
    finish(early[:2])
    for c in range(cands):
        early[2 + c].wait()
        low = dot(h_v[c], dn[...]).astype(BF)
        low_part[:, c] = low.reshape(n, seq // n, 2 * R)
    low_sum = Reduce(n, low_part, low_slots, low_full, links.at[0])
    low_sum.scatter()
    seed_copies = spread(
        "dp", dp, lambda peer: seeds, lambda k: seeds_all.at[spot], seed_links.at[0], seed_links.at[1]
    )
    finish(kv_copies)
    pending = low_sum
    for b in range(cands):
        if b:
            build_mask(seg, mask, b)
        finish(tok[b])
        for g in range(kv_count):
            attend(b, g, repeats, q_v, c_v, k_v, v_v, mask, vsum, dq_t, vg)
            if g == 0:
                pending.gather()
        if b == 0:
            finish(late)
        back_q, back_v = back_partial(b, kv_count, upq, upv, dq_t, vg)
        back = jnp.concatenate([back_q, back_v], axis=0).astype(BF)
        pending.done()
        back_part[b] = back.reshape(n, 2 * R // n, seq)
        pending = Reduce(
            n, back_part.at[b], back_slots.at[b], back_full.at[b], links.at[b + 1]
        )
        pending.scatter()
    low = [low_full[:, b].reshape(seq, 2 * R) for b in range(cands)]
    sums[...] = jnp.zeros_like(sums)
    ids = tile[...] * KB + block[...]
    ids_v = tile_v[:, kv_cols] * KB + block_v[:, kv_cols]
    ids_s[...] = ids
    add_upq(sums, ids_s, dq_t, low)
    pending.gather()
    add_upv(sums, ids_v, vg, low)
    for b in range(cands - 1):
        whole = back_full[b].reshape(2 * R, seq)
        for lo in range(0, width, 512):
            cols = slice(lo, lo + 512)
            grads0[b, :, cols] = dot(whole, h_v[b, :, cols]).astype(BF)
    pending.done()
    add_down(sums, ids_s, h_v, grads0, back_full[cands - 1].reshape(2 * R, seq))
    rows = KB // n
    for b in range(cands):
        feats[:, b] = project(sums, bank, b).reshape(n, rows, PB)
    tail = links.at[cands + 1]
    finish(spread(
        "mp", n, lambda peer: feats.at[peer], lambda k: feat_slots.at[k - 1], tail.at[0], tail.at[1]
    ))
    total = feats[m]
    for k in range(1, n):
        total += feat_slots[k - 1]
    flat = jnp.concatenate(
        [
            jnp.concatenate([total[b, i : i + 1] for i in range(rows)], axis=1)
            for b in range(cands)
        ],
        axis=0,
    )
    square = jnp.sum(flat * flat, axis=1, keepdims=True)
    finish(seed_copies)
    outs = pack.shape[2] // 2
    number = dot_nt(flat.astype(BF), seeds_all[...].reshape(n * outs, rows * PB))
    for j in range(n):
        pack[j, :, :outs] = number[:, j * outs : (j + 1) * outs]
        pack[j, :, outs:] = jnp.broadcast_to(square, (cands, outs))
    finish(spread(
        "mp", n, lambda peer: pack.at[peer], lambda k: pack_slots.at[k - 1], tail.at[2], tail.at[3]
    ))
    both = pack[m]
    for k in range(1, n):
        both += pack_slots[k - 1]
    out[...] = both


CHUNK = 256


def bucket_add(sums, ids, grads, transposed):
    buckets = sums.shape[0]
    spots = lax.broadcasted_iota(jnp.int32, (buckets, ids.shape[1]), 0)
    hot = jnp.where(spots == ids, 1.0, 0.0).astype(BF)
    sums[...] += (dot_nt if transposed else dot)(hot, grads)


def add_upq(sums, ids, dq_t, low):
    cands, width = dq_t.shape[0], dq_t.shape[1]
    chunk = min(CHUNK, width)

    def step(i, carry):
        rows = pl.ds(pl.multiple_of(i * chunk, chunk), chunk)
        grads = [dot(dq_t[b, rows, :], low[b][:, :R]) for b in range(cands)]
        bucket_add(sums, ids[2:3, rows], jnp.concatenate(grads, axis=1).astype(BF), False)
        return carry

    lax.fori_loop(0, width // chunk, step, 0)


def add_upv(sums, ids, vg, low):
    cands, width = vg.shape[0], vg.shape[2]
    grads = [dot(vg[b].T, low[b][:, R:]) for b in range(cands)]
    bucket_add(sums, ids, jnp.concatenate(grads, axis=1).astype(BF), False)


def add_down(sums, ids, h_v, grads0, back):
    cands, width = h_v.shape[0], h_v.shape[2]
    chunk = min(CHUNK, width)

    def step(i, carry):
        cols = pl.ds(pl.multiple_of(i * chunk, chunk), chunk)
        grads = [grads0[b, :, cols] for b in range(cands - 1)]
        grads.append(dot(back, h_v[cands - 1, :, cols]).astype(BF))
        for j in range(2):
            part = jnp.concatenate([grad[j * R : (j + 1) * R] for grad in grads], axis=0)
            bucket_add(sums, ids[j : j + 1, cols], part, True)
        return carry

    lax.fori_loop(0, width // chunk, step, 0)


def project(sums, bank, b):
    total = jnp.zeros((KB, PB), F32)
    for t in range(NT):
        part = sums[t * KB : (t + 1) * KB, b * R : (b + 1) * R].astype(BF)
        total += dot(part, bank[t])
    return total


ANY = pl.BlockSpec(memory_space=pl.ANY)
VMEM = pl.BlockSpec(memory_space=pltpu.VMEM)


def local(
    hidden_in, query_act, key_act, value_act, ctx_grad, segment_ids,
    down_query, up_query, down_value, up_value,
    block_rows, tile_rows, block_value, tile_value, tile_bank, seed_feats,
):
    cands, seq, width = query_act.shape
    heads = width // DH
    kv_count = max(heads // (H // KVH), 1)
    repeats = heads // kv_count
    kvw = kv_count * DH
    n, dp = lax.axis_size("mp"), lax.axis_size("dp")
    outs = seed_feats.shape[0] * dp // n
    hop = [pltpu.VMEM((n, cands, seq // n, 2 * R), BF), pltpu.VMEM((n - 1, cands, seq // n, 2 * R), BF)]
    fold = (2 * R // n, seq)
    both = pl.pallas_call(
        functools.partial(main_kernel, n, dp, kv_count, repeats),
        out_shape=jax.ShapeDtypeStruct((cands, 2 * outs), F32),
        in_specs=[ANY] * 5 + [VMEM] + [ANY] * 4 + [VMEM] * 6,
        out_specs=VMEM,
        scratch_shapes=[
            pltpu.VMEM((cands, seq, width), BF),
            pltpu.VMEM((cands, seq, width), BF),
            pltpu.VMEM((cands, seq, width), BF),
            pltpu.VMEM((cands, seq, kvw), BF),
            pltpu.VMEM((cands, seq, kvw), BF),
            pltpu.VMEM((width, 2 * R), BF),
            pltpu.VMEM((R, width), BF),
            pltpu.VMEM((R, kvw), BF),
            pltpu.VMEM((seq, seq), F32),
            pltpu.VMEM((seq, DH), F32),
            pltpu.VMEM((cands, width, seq), BF),
            pltpu.VMEM((cands, seq, kvw), BF),
            pltpu.VMEM((KB * NT, cands * R), F32),
            pltpu.VMEM((max(cands - 1, 1), 2 * R, width), BF),
            pltpu.VMEM(block_rows.shape, jnp.int32),
            hop[0], hop[1], hop[0],
            pltpu.VMEM((cands, n) + fold, BF),
            pltpu.VMEM((cands, n - 1) + fold, BF),
            pltpu.VMEM((cands, n) + fold, BF),
            pltpu.VMEM((n, cands, KB // n, PB), F32),
            pltpu.VMEM((n - 1, cands, KB // n, PB), F32),
            pltpu.VMEM((n, cands, 2 * outs), F32),
            pltpu.VMEM((n - 1, cands, 2 * outs), F32),
            pltpu.VMEM((dp,) + seed_feats.shape, BF),
            pltpu.SemaphoreType.DMA((6 + 3 * cands,)),
            pltpu.SemaphoreType.DMA((cands + 2, 4, n - 1)),
            pltpu.SemaphoreType.DMA((2, dp - 1)),
        ],
        compiler_params=pltpu.CompilerParams(
            vmem_limit_bytes=56 << 20, collective_id=0, has_side_effects=True
        ),
        cost_estimate=pl.CostEstimate(
            flops=cands * heads * seq * seq * DH * 12, bytes_accessed=16 << 20,
            transcendentals=cands * heads * seq * seq,
        ),
        name="gradient_features",
    )(hidden_in, query_act, key_act, value_act, ctx_grad, segment_ids,
      down_query, up_query, down_value, up_value,
      block_rows, tile_rows, block_value[None], tile_value[None], tile_bank, seed_feats)
    return both[:, :outs] * lax.rsqrt(both[:, outs:] / K + EPS) * K ** (-0.5)


def solution(mesh):
    return jax.shard_map(
        local,
        mesh=mesh,
        in_specs=(
            P("dp", None, "mp"),
            P("dp", None, "mp"),
            P("dp", None, None),
            P("dp", None, None),
            P("dp", None, "mp"),
            P("dp", None),
            P("mp", None),
            P(None, "mp"),
            P("mp", None),
            P(),
            P(None, "mp"),
            P(None, "mp"),
            P(),
            P(),
            P(),
            P("dp", "mp"),
        ),
        out_specs=P("dp", "mp"),
        check_vma=False,
    )
```

```python
import functools
import math

import jax
import jax.numpy as jnp
from jax import lax
from jax.experimental import pallas as pl
from jax.experimental.pallas import tpu as pltpu
from jax.sharding import PartitionSpec as P

H = 64
KVH = 8
DH = 128
R = 128
K = 8192
PB = 128
NT = 8
KB = K // PB
REACH = 256

EPS = 1e-06
BF = jnp.bfloat16
F32 = jnp.float32
NEG = -1e30


def dot(a, b):
    return jnp.dot(a, b, preferred_element_type=F32)


def dot_nt(a, b):
    return lax.dot_general(a, b, (((1,), (1,)), ((), ())), preferred_element_type=F32)


def build_mask(seg_ref, mask_ref, b):
    seq = mask_ref.shape[0]
    row = seg_ref[b : b + 1, :].astype(F32)
    column = jnp.broadcast_to(row, (128, seq)).T[:, :1]
    for lo in range(0, seq, REACH):
        shape = (seq, REACH)
        key_pos = lax.broadcasted_iota(jnp.int32, shape, 0)
        query_pos = lax.broadcasted_iota(jnp.int32, shape, 1) + lo
        same = column == row[:, lo : lo + REACH]
        allowed = jnp.logical_and(key_pos <= query_pos, same)
        mask_ref[:, lo : lo + REACH] = jnp.where(allowed, 0.0, NEG)


UNROLL = 4


def attend(b, g, repeats, q_v, c_v, k_v, v_v, mask, vsum, dq_t, vg):
    seq = mask.shape[0]
    kv_cols = slice(g * DH, (g + 1) * DH)
    keys = k_v[b, :, kv_cols]
    vals = v_v[b, :, kv_cols]
    keys_t = keys.T
    scale = 1.0 / math.sqrt(DH)
    vsum[...] = jnp.zeros_like(vsum)

    units = [(j, lo) for j in range(UNROLL) for lo in range(0, seq, REACH)]

    def heads(i, carry):
        cols = [
            pl.ds(pl.multiple_of((g * repeats + i * UNROLL + j) * DH, DH), DH)
            for j in range(UNROLL)
        ]

        def span(lo):
            return slice(max(lo - REACH, 0), lo + REACH)

        def products(j, lo):
            quer = q_v[b, lo : lo + REACH, cols[j]]
            cot = c_v[b, lo : lo + REACH, cols[j]]
            return dot_nt(keys[span(lo)], quer), dot_nt(vals[span(lo)], cot)

        def soft(lo, logits, prob_grads):
            first, last = span(lo).start, span(lo).stop
            probs, grads = [], []
            for at in range(lo, lo + REACH, DH):
                low, high = max(at - REACH, 0), at + DH
                rows, lanes = slice(low - first, high - first), slice(at - lo, at - lo + DH)
                logit = logits[rows, lanes] + mask[low:high, at : at + DH]
                prob_grad = prob_grads[rows, lanes]
                top = jnp.max(logit, axis=0, keepdims=True)
                terms = jnp.exp2((logit - top) * (scale * math.log2(math.e)))
                inv = 1.0 / jnp.sum(terms, axis=0, keepdims=True)
                delta = jnp.sum(terms * prob_grad, axis=0, keepdims=True) * inv
                prob = terms * inv

                def padded(block):
                    above = jnp.zeros((low - first, DH), BF)
                    below = jnp.zeros((last - high, DH), BF)
                    parts = [p for p in (above, block.astype(BF), below) if p.shape[0]]
                    return jnp.concatenate(parts, axis=0) if len(parts) > 1 else parts[0]

                probs.append(padded(prob))
                grads.append(padded(prob * (prob_grad - delta)))
            return jnp.concatenate(probs, axis=1), jnp.concatenate(grads, axis=1)

        held = {}
        ready = products(*units[0])
        for at, (j, lo) in enumerate(units):
            logits, prob_grads = ready
            if at + 1 < len(units):
                ready = products(*units[at + 1])
            probs, grads = soft(lo, logits, prob_grads)
            held[j, lo] = probs
            dq = dot(keys_t[:, span(lo)], grads) * scale
            dq_t[b, cols[j], lo : lo + REACH] = dq.astype(BF)
        for lo in range(0, seq, REACH):
            probs = jnp.concatenate([held[j, lo] for j in range(UNROLL)], axis=1)
            cots = jnp.concatenate(
                [c_v[b, lo : lo + REACH, cols[j]] for j in range(UNROLL)], axis=0
            )
            vsum[span(lo), :] += dot(probs, cots)
        return carry

    lax.fori_loop(0, repeats // UNROLL, heads, 0)
    vg[b, :, kv_cols] = vsum[...].astype(BF)


def back_partial(b, kv_count, upq, upv, dq_t, vg):
    back_q = dot(upq[...], dq_t[b])
    back_v = jnp.zeros((R, vg.shape[1]), F32)
    for g in range(kv_count):
        cols = slice(g * DH, (g + 1) * DH)
        back_v += dot_nt(upv[:, cols], vg[b, :, cols])
    return back_q, back_v


MESH = pl.DeviceIdType.MESH


def device(axis, peer):
    if axis == "dp":
        return (peer, lax.axis_index("mp"))
    return (lax.axis_index("dp"), peer)


def meet(sizes):
    barrier = pltpu.get_barrier_semaphore()
    for axis, n in sizes:
        me = lax.axis_index(axis)
        for k in range(1, n):
            peer = device(axis, lax.rem(me + k, n))
            pl.semaphore_signal(barrier, inc=1, device_id=peer, device_id_type=MESH)
    pl.semaphore_wait(barrier, sum(n - 1 for _, n in sizes))


def spread(axis, n, source, target, send, recv):
    me = lax.axis_index(axis)
    copies = []
    for k in range(1, n):
        peer = lax.rem(me + k, n)
        copy = pltpu.make_async_remote_copy(
            src_ref=source(peer),
            dst_ref=target(k),
            send_sem=send.at[k - 1],
            recv_sem=recv.at[k - 1],
            device_id=device(axis, peer),
            device_id_type=MESH,
        )
        copy.start()
        copies.append(copy)
    return copies


def finish(copies):
    for copy in copies:
        copy.wait()


class Reduce:
    def __init__(self, n, part, slots, full, sems):
        self.n, self.part, self.slots, self.full, self.sems = n, part, slots, full, sems

    def scatter(self):
        self.first = spread(
            "mp", self.n, lambda peer: self.part.at[peer], lambda k: self.slots.at[k - 1],
            self.sems.at[0], self.sems.at[1],
        )

    def gather(self):
        finish(self.first)
        me = lax.axis_index("mp")
        total = self.part[me].astype(F32)
        for k in range(1, self.n):
            total += self.slots[k - 1].astype(F32)
        self.full[me] = total.astype(BF)
        self.second = spread(
            "mp", self.n, lambda peer: self.full.at[me], lambda k: self.full.at[me],
            self.sems.at[2], self.sems.at[3],
        )

    def done(self):
        finish(self.second)


def main_kernel(
    n, dp, kv_count, repeats,
    hid, que, key, val, ctx, seg, downq, upq_h, downv, upv_h,
    block, tile, block_v, tile_v, bank, seeds,
    out,
    h_v, q_v, c_v, k_v, v_v, dn, upq, upv, mask, vsum, dq_t, vg, sums, grads0, ids_s,
    low_part, low_slots, low_full, back_part, back_slots, back_full,
    feats, feat_slots, pack, pack_slots, seeds_all, sems, links, seed_links,
):
    m = lax.axis_index("mp")
    heads = kv_count * repeats
    kv_first = m * heads // (H // KVH)
    kv_cols = pl.ds(pl.multiple_of(kv_first * DH, DH), kv_count * DH)
    cands, seq, width = que.shape
    count = [0]

    def load(src, dst):
        copy = pltpu.make_async_copy(src, dst, sems.at[count[0]])
        count[0] += 1
        copy.start()
        return copy

    early = [load(downq, dn.at[:, :R]), load(downv, dn.at[:, R:])]
    early += [load(hid.at[b], h_v.at[b]) for b in range(cands)]
    kv_copies = [load(key.at[:, :, kv_cols], k_v), load(val.at[:, :, kv_cols], v_v)]
    tok = [[load(que.at[b], q_v.at[b]), load(ctx.at[b], c_v.at[b])] for b in range(cands)]
    late = [load(upq_h, upq), load(upv_h.at[:, kv_cols], upv)]

    build_mask(seg, mask, 0)
    spot = lax.axis_index("dp")
    seeds_all[spot] = seeds[...]
    meet((("mp", n), ("dp", dp)))
    finish(early[:2])
    for c in range(cands):
        early[2 + c].wait()
        low = dot(h_v[c], dn[...]).astype(BF)
        low_part[:, c] = low.reshape(n, seq // n, 2 * R)
    low_sum = Reduce(n, low_part, low_slots, low_full, links.at[0])
    low_sum.scatter()
    seed_copies = spread(
        "dp", dp, lambda peer: seeds, lambda k: seeds_all.at[spot], seed_links.at[0], seed_links.at[1]
    )
    finish(kv_copies)
    pending = low_sum
    for b in range(cands):
        if b:
            build_mask(seg, mask, b)
        finish(tok[b])
        for g in range(kv_count):
            attend(b, g, repeats, q_v, c_v, k_v, v_v, mask, vsum, dq_t, vg)
            if g == 0:
                pending.gather()
        if b == 0:
            finish(late)
        back_q, back_v = back_partial(b, kv_count, upq, upv, dq_t, vg)
        back = jnp.concatenate([back_q, back_v], axis=0).astype(BF)
        pending.done()
        back_part[b] = back.reshape(n, 2 * R // n, seq)
        pending = Reduce(
            n, back_part.at[b], back_slots.at[b], back_full.at[b], links.at[b + 1]
        )
        pending.scatter()
    low = [low_full[:, b].reshape(seq, 2 * R) for b in range(cands)]
    sums[...] = jnp.zeros_like(sums)
    ids = tile[...] * KB + block[...]
    ids_v = tile_v[:, kv_cols] * KB + block_v[:, kv_cols]
    ids_s[...] = ids
    add_upq(sums, ids_s, dq_t, low)
    pending.gather()
    add_upv(sums, ids_v, vg, low)
    for b in range(cands - 1):
        whole = back_full[b].reshape(2 * R, seq)
        for lo in range(0, width, 512):
            cols = slice(lo, lo + 512)
            grads0[b, :, cols] = dot(whole, h_v[b, :, cols]).astype(BF)
    pending.done()
    add_down(sums, ids_s, h_v, grads0, back_full[cands - 1].reshape(2 * R, seq))
    rows = KB // n
    for b in range(cands):
        feats[:, b] = project(sums, bank, b).reshape(n, rows, PB)
    tail = links.at[cands + 1]
    finish(spread(
        "mp", n, lambda peer: feats.at[peer], lambda k: feat_slots.at[k - 1], tail.at[0], tail.at[1]
    ))
    total = feats[m]
    for k in range(1, n):
        total += feat_slots[k - 1]
    flat = jnp.concatenate(
        [
            jnp.concatenate([total[b, i : i + 1] for i in range(rows)], axis=1)
            for b in range(cands)
        ],
        axis=0,
    )
    square = jnp.sum(flat * flat, axis=1, keepdims=True)
    finish(seed_copies)
    outs = pack.shape[2] // 2
    number = dot_nt(flat.astype(BF), seeds_all[...].reshape(n * outs, rows * PB))
    for j in range(n):
        pack[j, :, :outs] = number[:, j * outs : (j + 1) * outs]
        pack[j, :, outs:] = jnp.broadcast_to(square, (cands, outs))
    finish(spread(
        "mp", n, lambda peer: pack.at[peer], lambda k: pack_slots.at[k - 1], tail.at[2], tail.at[3]
    ))
    both = pack[m]
    for k in range(1, n):
        both += pack_slots[k - 1]
    out[...] = both


CHUNK = 512


def bucket_add(sums, ids, grads, transposed):
    buckets = sums.shape[0]
    spots = lax.broadcasted_iota(jnp.int32, (buckets, ids.shape[1]), 0)
    hot = jnp.where(spots == ids, 1.0, 0.0).astype(BF)
    sums[...] += (dot_nt if transposed else dot)(hot, grads)


def add_upq(sums, ids, dq_t, low):
    cands, width = dq_t.shape[0], dq_t.shape[1]
    chunk = min(CHUNK, width)

    def step(i, carry):
        rows = pl.ds(pl.multiple_of(i * chunk, chunk), chunk)
        grads = [dot(dq_t[b, rows, :], low[b][:, :R]) for b in range(cands)]
        bucket_add(sums, ids[2:3, rows], jnp.concatenate(grads, axis=1).astype(BF), False)
        return carry

    lax.fori_loop(0, width // chunk, step, 0)


def add_upv(sums, ids, vg, low):
    cands, width = vg.shape[0], vg.shape[2]
    grads = [dot(vg[b].T, low[b][:, R:]) for b in range(cands)]
    bucket_add(sums, ids, jnp.concatenate(grads, axis=1).astype(BF), False)


def add_down(sums, ids, h_v, grads0, back):
    cands, width = h_v.shape[0], h_v.shape[2]
    chunk = min(CHUNK, width)

    def step(i, carry):
        cols = pl.ds(pl.multiple_of(i * chunk, chunk), chunk)
        grads = [grads0[b, :, cols] for b in range(cands - 1)]
        grads.append(dot(back, h_v[cands - 1, :, cols]).astype(BF))
        for j in range(2):
            part = jnp.concatenate([grad[j * R : (j + 1) * R] for grad in grads], axis=0)
            bucket_add(sums, ids[j : j + 1, cols], part, True)
        return carry

    lax.fori_loop(0, width // chunk, step, 0)


def project(sums, bank, b):
    total = jnp.zeros((KB, PB), F32)
    for t in range(NT):
        part = sums[t * KB : (t + 1) * KB, b * R : (b + 1) * R].astype(BF)
        total += dot(part, bank[t])
    return total


ANY = pl.BlockSpec(memory_space=pl.ANY)
VMEM = pl.BlockSpec(memory_space=pltpu.VMEM)


def local(
    hidden_in, query_act, key_act, value_act, ctx_grad, segment_ids,
    down_query, up_query, down_value, up_value,
    block_rows, tile_rows, block_value, tile_value, tile_bank, seed_feats,
):
    cands, seq, width = query_act.shape
    heads = width // DH
    kv_count = max(heads // (H // KVH), 1)
    repeats = heads // kv_count
    kvw = kv_count * DH
    n, dp = lax.axis_size("mp"), lax.axis_size("dp")
    outs = seed_feats.shape[0] * dp // n
    hop = [pltpu.VMEM((n, cands, seq // n, 2 * R), BF), pltpu.VMEM((n - 1, cands, seq // n, 2 * R), BF)]
    fold = (2 * R // n, seq)
    both = pl.pallas_call(
        functools.partial(main_kernel, n, dp, kv_count, repeats),
        out_shape=jax.ShapeDtypeStruct((cands, 2 * outs), F32),
        in_specs=[ANY] * 5 + [VMEM] + [ANY] * 4 + [VMEM] * 6,
        out_specs=VMEM,
        scratch_shapes=[
            pltpu.VMEM((cands, seq, width), BF),
            pltpu.VMEM((cands, seq, width), BF),
            pltpu.VMEM((cands, seq, width), BF),
            pltpu.VMEM((cands, seq, kvw), BF),
            pltpu.VMEM((cands, seq, kvw), BF),
            pltpu.VMEM((width, 2 * R), BF),
            pltpu.VMEM((R, width), BF),
            pltpu.VMEM((R, kvw), BF),
            pltpu.VMEM((seq, seq), F32),
            pltpu.VMEM((seq, DH), F32),
            pltpu.VMEM((cands, width, seq), BF),
            pltpu.VMEM((cands, seq, kvw), BF),
            pltpu.VMEM((KB * NT, cands * R), F32),
            pltpu.VMEM((max(cands - 1, 1), 2 * R, width), BF),
            pltpu.VMEM(block_rows.shape, jnp.int32),
            hop[0], hop[1], hop[0],
            pltpu.VMEM((cands, n) + fold, BF),
            pltpu.VMEM((cands, n - 1) + fold, BF),
            pltpu.VMEM((cands, n) + fold, BF),
            pltpu.VMEM((n, cands, KB // n, PB), F32),
            pltpu.VMEM((n - 1, cands, KB // n, PB), F32),
            pltpu.VMEM((n, cands, 2 * outs), F32),
            pltpu.VMEM((n - 1, cands, 2 * outs), F32),
            pltpu.VMEM((dp,) + seed_feats.shape, BF),
            pltpu.SemaphoreType.DMA((6 + 3 * cands,)),
            pltpu.SemaphoreType.DMA((cands + 2, 4, n - 1)),
            pltpu.SemaphoreType.DMA((2, dp - 1)),
        ],
        compiler_params=pltpu.CompilerParams(
            vmem_limit_bytes=56 << 20, collective_id=0, has_side_effects=True
        ),
        cost_estimate=pl.CostEstimate(
            flops=cands * heads * seq * seq * DH * 12, bytes_accessed=16 << 20,
            transcendentals=cands * heads * seq * seq,
        ),
        name="gradient_features",
    )(hidden_in, query_act, key_act, value_act, ctx_grad, segment_ids,
      down_query, up_query, down_value, up_value,
      block_rows, tile_rows, block_value[None], tile_value[None], tile_bank, seed_feats)
    return both[:, :outs] * lax.rsqrt(both[:, outs:] / K + EPS) * K ** (-0.5)


def solution(mesh):
    return jax.shard_map(
        local,
        mesh=mesh,
        in_specs=(
            P("dp", None, "mp"),
            P("dp", None, "mp"),
            P("dp", None, None),
            P("dp", None, None),
            P("dp", None, "mp"),
            P("dp", None),
            P("mp", None),
            P(None, "mp"),
            P("mp", None),
            P(),
            P(None, "mp"),
            P(None, "mp"),
            P(),
            P(),
            P(),
            P("dp", "mp"),
        ),
        out_specs=P("dp", "mp"),
        check_vma=False,
    )
```
